32 devices in a mesh: ctx: 8 (over z, y), head: 4 (over x, core).
Axes of the slice: x: 2, y: 2, z: 4, core: 2. Of those that a mesh axis runs over, the one named last changes fastest.
Arguments:
- delta_q: bfloat16 [2048, 2048], P('ctx', 'head'), may hold values from -6 to 6
- delta_k: bfloat16 [2048, 2048], P('ctx', 'head'), may hold values from -6 to 6
- delta_v: bfloat16 [2048, 2048], P('ctx', 'head'), may hold values from -6 to 6
- beta: float32 [2048, 16], P('ctx', 'head'), may hold values from 0 to 0.9, as said below
- log_decay: float32 [2048, 16], P('ctx', 'head'), may hold values from -1 to 0, as said below
- out_gate: bfloat16 [2048, 2048], P('ctx', 'head'), may hold values from -6 to 6
- norm_gain: float32 [128], replicated, may hold values from 0.1 to 1.9
- attn_q: bfloat16 [2048, 2048], P('ctx', 'head'), may hold values from -16 to 16
- attn_k: bfloat16 [2048, 2048], P('ctx', 'head'), may hold values from -16 to 16
- attn_v: bfloat16 [2048, 2048], P('ctx', 'head'), may hold values from -6 to 6
- w_delta_out: bfloat16 [2048, 2048], P('head'), may hold values from -0.125 to 0.125
- w_attn_out: bfloat16 [2048, 2048], P('head'), may hold values from -0.125 to 0.125
Outputs:
- branch_sum: bfloat16 [2048, 2048], P(('ctx', 'head'))
The draws below stay inside these ranges and needn't reach their ends.
Inputs may be any that keep to these rules, and one draw needn't show every extreme that they name: `beta`: write strengths, positive. `log_decay`: log decays, negative.
All inputs are finite; a program needn't handle non-finite values.
Results may differ from the reference program's by a relative error of at most 0.022.
Values may be sent and summed in bfloat16 or wider, within the bound.
A program may use at most 128 MiB of HBM per device.

```python
import math
import jax
import jax.numpy as jnp
from jax import lax

D = 2048
H = 16
DH = 128
WINDOW = 1024
TOKENS_PER_PART = 256
SEQUENCE_TOKENS = 2048
N_HEAD = 4


def speeds_of_heads(key):
    return jax.random.uniform(jax.random.fold_in(key, 11), (H,), jnp.float32)


def draw_beta(key, part):
    head_speed = speeds_of_heads(key)
    fast_log = math.log(0.6)
    slow_log = math.log(0.5 * DH / SEQUENCE_TOKENS)
    base_rate = jnp.exp(fast_log * (1.0 - head_speed) + slow_log * head_speed)
    roughness = jax.random.uniform(jax.random.fold_in(key, 16), (SEQUENCE_TOKENS, H), jnp.float32, 0.5, 1.5)
    return jnp.minimum(base_rate[None, :] * roughness, 0.9)


def draw_log_decay(key, part):
    head_speed = speeds_of_heads(key)
    fast_log = math.log(1.0 / 40.0)
    slow_log = math.log(0.5 / SEQUENCE_TOKENS)
    base_rate = jnp.exp(fast_log * (1.0 - head_speed) + slow_log * head_speed)
    device_scale = jnp.exp(jax.random.uniform(jax.random.fold_in(key, 12), (SEQUENCE_TOKENS // TOKENS_PER_PART, H), jnp.float32, -math.log(2.0), math.log(2.0)))
    device_scale = jnp.repeat(device_scale, TOKENS_PER_PART, axis=0)
    roughness = jax.random.uniform(jax.random.fold_in(key, 13), (SEQUENCE_TOKENS, H), jnp.float32, 0.5, 1.5)
    steady = -base_rate[None, :] * device_scale * roughness
    transfer_groups = jax.random.randint(jax.random.fold_in(key, 14), (3,), 0, SEQUENCE_TOKENS)
    masked_entries = jnp.any(jnp.arange(SEQUENCE_TOKENS)[:, None] == transfer_groups[None, :], axis=1)
    sudden = jnp.log(jax.random.uniform(jax.random.fold_in(key, 15), (SEQUENCE_TOKENS, H), jnp.float32, 0.5, 0.8))
    return jnp.where(masked_entries[:, None], sudden, steady)


def draw_attn_q(key, part):
    shape = (SEQUENCE_TOKENS, H * DH)
    return jnp.clip(jax.random.normal(jax.random.fold_in(key, 21), shape, jnp.float32), -4.0, 4.0).astype(jnp.bfloat16)


def draw_attn_k(key, part):
    shape = (SEQUENCE_TOKENS, H * DH)
    return jnp.clip(jax.random.normal(jax.random.fold_in(key, 22), shape, jnp.float32), -4.0, 4.0).astype(jnp.bfloat16)


def steps_of(key, dims, cuts, smallest, top_value):
    def one(dim, blocks):
        heights = jax.random.uniform(jax.random.fold_in(jax.random.fold_in(key, 6), dim), (blocks,), jnp.float32, smallest / len(cuts), top_value / len(cuts))
        return jnp.repeat(jnp.exp(heights), dims[dim] // blocks).reshape((-1,) + (1,) * (len(dims) - dim - 1))

    level = one(*cuts[0])
    for cut in cuts[1:]:
        level = level * one(*cut)
    return level


def centred(stream_key, extent, deviation, most, shards=(), kind=jnp.bfloat16):
    values = jax.random.normal(stream_key, extent, jnp.float32) * deviation
    if len(shards) > 0:
        values = steps_of(stream_key, extent, shards, -0.22, 0.18) * values
    return jnp.clip(values, min=-most, max=most).astype(kind)


def setup_inputs(seed: int = 0) -> dict:
    keys = jax.random.split(jax.random.key(seed), 13)
    delta_q = centred(keys[0], (SEQUENCE_TOKENS, H * DH), 1.0, 6.0, ((0, 8), (1, 4)))
    delta_k = centred(keys[1], (SEQUENCE_TOKENS, H * DH), 1.0, 6.0, ((0, 8), (1, 4)))
    delta_v = centred(keys[2], (SEQUENCE_TOKENS, H * DH), 1.0, 6.0, ((0, 8), (1, 4)))
    beta = draw_beta(jax.random.fold_in(keys[12], 71), 0)
    log_decay = draw_log_decay(jax.random.fold_in(keys[12], 71), 0)
    out_gate = centred(keys[5], (SEQUENCE_TOKENS, H * DH), 1.0, 6.0, ((0, 8), (1, 4)))
    norm_gain = jnp.clip(1.0 + 0.18 * jax.random.normal(keys[6], (DH,), jnp.float32), 0.1, 1.9)
    attn_q = draw_attn_q(jax.random.fold_in(keys[12], 71), 0)
    attn_k = draw_attn_k(jax.random.fold_in(keys[12], 71), 0)
    attn_v = centred(keys[9], (SEQUENCE_TOKENS, H * DH), 1.0, 6.0, ((0, 8), (1, 4)))
    w_delta_out = centred(keys[10], (H * DH, D), (H * DH) ** -0.5, 0.125, ((0, 4),))
    w_attn_out = centred(keys[11], (H * DH, D), (H * DH) ** -0.5, 0.125, ((0, 4),))
    return {"delta_q": delta_q, "delta_k": delta_k, "delta_v": delta_v, "beta": beta, "log_decay": log_decay, "out_gate": out_gate, "norm_gain": norm_gain, "attn_q": attn_q, "attn_k": attn_k, "attn_v": attn_v, "w_delta_out": w_delta_out, "w_attn_out": w_attn_out}


highest = lax.Precision.HIGHEST

def unit_rows(array):
    return array / jnp.sqrt(lax.optimization_barrier(jnp.sum(array * array, axis=-1, keepdims=True)) + 1e-06)

def unit_inverse(lower_part):
    order_len = lower_part.shape[-1]
    identity = jnp.eye(order_len, dtype=jnp.float32)
    powered = -lower_part
    result = identity + powered
    for counter in range(1, max(1, (order_len - 1).bit_length())):
        powered = jnp.matmul(powered, powered, precision=highest)
        result = jnp.matmul(result, identity + powered, precision=highest)
    return result

def block_terms(queries, keys_in, values_in, betas, log_rates):
    cumulative = jnp.cumsum(log_rates, axis=-1)
    length = queries.shape[-2]
    positions = jnp.arange(length)
    strict = positions[:, None] > positions[None, :]
    inclusive = positions[:, None] >= positions[None, :]
    spread = cumulative[..., :, None] - cumulative[..., None, :]
    ratio_strict = jnp.where(strict, jnp.exp(jnp.where(strict, spread, 0.0)), 0.0)
    ratio_incl = jnp.where(inclusive, jnp.exp(jnp.where(inclusive, spread, 0.0)), 0.0)
    key_gram = jnp.einsum('...td,...sd->...ts', keys_in, keys_in, precision=highest)
    inverse = unit_inverse(betas[..., :, None] * ratio_strict * key_gram)
    decayed = jnp.exp(cumulative)
    pseudo = jnp.matmul(inverse, betas[..., None] * values_in, precision=highest)
    writer = jnp.matmul(inverse, (betas * decayed)[..., None] * keys_in, precision=highest)
    to_end = jnp.exp(cumulative[..., -1:] - cumulative)
    keys_end = keys_in * to_end[..., None]
    identity = jnp.eye(queries.shape[-1], dtype=jnp.float32)
    transition = jnp.exp(cumulative[..., -1])[..., None, None] * identity - jnp.einsum('...td,...te->...de', keys_end, writer, precision=highest)
    contrib = jnp.einsum('...td,...te->...de', keys_end, pseudo, precision=highest)
    mixing = ratio_incl * jnp.einsum('...td,...sd->...ts', queries, keys_in, precision=highest)
    local_out = jnp.matmul(mixing, pseudo, precision=highest)
    carry_out = decayed[..., None] * queries - jnp.matmul(mixing, writer, precision=highest)
    return (transition, contrib, local_out, carry_out)

def window_block(queries, keys_in, values_in, query_pos, key_pos):
    scores = jnp.einsum('thd,shd->hts', queries.astype(jnp.float32), keys_in.astype(jnp.float32)) * DH ** (-0.5)
    offsets = query_pos[:, None] - key_pos[None, :]
    inside = (offsets >= 0) & (offsets < WINDOW) & (key_pos[None, :] >= 0)
    masked = jnp.where(inside[None], scores, -1e+30)
    block_max = lax.optimization_barrier(jnp.max(masked, axis=-1))
    weights = jnp.where(inside[None], jnp.exp(masked - block_max[..., None]), 0.0)
    probs = weights.astype(jnp.bfloat16)
    block_num = jnp.einsum('hts,shd->htd', probs.astype(jnp.float32), values_in.astype(jnp.float32))
    block_den = lax.optimization_barrier(jnp.sum(weights, axis=-1))
    return (block_max, block_num, block_den)

def group_sum(delta_heads, w_delta, attn_heads, w_attn):
    columns = H * DH // N_HEAD
    total = jnp.zeros((delta_heads.shape[0], w_delta.shape[1]), jnp.float32)
    for group in range(N_HEAD):
        low = group * columns
        high = (group + 1) * columns
        partial_term = jnp.dot(delta_heads[:, low:high], w_delta[low:high], preferred_element_type=jnp.float32)
        partial_term = partial_term + jnp.dot(attn_heads[:, low:high], w_attn[low:high], preferred_element_type=jnp.float32)
        rounded = partial_term.astype(jnp.bfloat16)
        total = total + lax.optimization_barrier(rounded).astype(jnp.float32)
    return total

def reference(delta_q, delta_k, delta_v, beta, log_decay, out_gate, norm_gain, attn_q, attn_k, attn_v, w_delta_out, w_attn_out):
    block_len = min(64, SEQUENCE_TOKENS)
    blocks = SEQUENCE_TOKENS // block_len

    def heads_blocks(array):
        return array.astype(jnp.float32).reshape(blocks, block_len, H, DH).transpose(0, 2, 1, 3)
    queries = unit_rows(heads_blocks(delta_q)) * DH ** (-0.5)
    keys_in = unit_rows(heads_blocks(delta_k))
    values_in = heads_blocks(delta_v)
    betas = beta.reshape(blocks, block_len, H).transpose(0, 2, 1)
    log_rates = log_decay.reshape(blocks, block_len, H).transpose(0, 2, 1)

    def advance(state, inputs):
        transition, contrib, local_out, carry_out = block_terms(*inputs)
        outputs = local_out + jnp.matmul(carry_out, state, precision=highest)
        return (jnp.matmul(transition, state, precision=highest) + contrib, outputs)
    initial = jnp.zeros((H, DH, DH), jnp.float32)
    final_state, delta_raw = lax.scan(advance, initial, (queries, keys_in, values_in, betas, log_rates))
    delta_raw = delta_raw.transpose(0, 2, 1, 3).reshape(SEQUENCE_TOKENS, H, DH)
    gate_act = jax.nn.silu(out_gate.astype(jnp.float32).reshape(SEQUENCE_TOKENS, H, DH))
    normed = delta_raw / jnp.sqrt(lax.optimization_barrier(jnp.mean(delta_raw * delta_raw, axis=-1, keepdims=True)) + 1e-06) * norm_gain * gate_act
    delta_heads = normed.reshape(SEQUENCE_TOKENS, H * DH).astype(jnp.bfloat16)
    span = WINDOW // TOKENS_PER_PART

    def attend(block_index):
        query_start = (block_index * TOKENS_PER_PART).astype(jnp.int32)
        query_rows = lax.dynamic_slice_in_dim(attn_q, query_start, TOKENS_PER_PART, 0).reshape(TOKENS_PER_PART, H, DH)
        query_pos = query_start + jnp.arange(TOKENS_PER_PART, dtype=jnp.int32)
        maxima, numers, denoms = ([], [], [])
        for back in range(span + 1):
            source = block_index - back
            key_start = (jnp.maximum(source, 0) * TOKENS_PER_PART).astype(jnp.int32)
            key_rows = lax.dynamic_slice_in_dim(attn_k, key_start, TOKENS_PER_PART, 0).reshape(TOKENS_PER_PART, H, DH)
            value_rows = lax.dynamic_slice_in_dim(attn_v, key_start, TOKENS_PER_PART, 0).reshape(TOKENS_PER_PART, H, DH)
            key_pos = (source * TOKENS_PER_PART).astype(jnp.int32) + jnp.arange(TOKENS_PER_PART, dtype=jnp.int32)
            block_max, block_num, block_den = window_block(query_rows, key_rows, value_rows, query_pos, key_pos)
            maxima.append(block_max)
            numers.append(block_num)
            denoms.append(block_den)
        top = maxima[0]
        for block_max in maxima[1:]:
            top = jnp.maximum(top, block_max)
        numer = jnp.zeros_like(numers[0])
        denom = jnp.zeros_like(denoms[0])
        for block_max, block_num, block_den in zip(maxima, numers, denoms):
            factor = jnp.exp(block_max - top)
            numer = numer + factor[..., None] * block_num
            denom = denom + factor * block_den
        result = numer / denom[..., None]
        return result.transpose(1, 0, 2).reshape(TOKENS_PER_PART, H * DH).astype(jnp.bfloat16)
    attn_heads = lax.map(attend, jnp.arange(SEQUENCE_TOKENS // TOKENS_PER_PART, dtype=jnp.int32)).reshape(SEQUENCE_TOKENS, H * DH)
    total = group_sum(delta_heads, w_delta_out, attn_heads, w_attn_out)
    return total.astype(jnp.bfloat16)
```

```python
import functools

import jax
import jax.numpy as jnp
from jax import lax
from jax.experimental import pallas as pl
from jax.experimental.pallas import tpu as pltpu
from jax.sharding import PartitionSpec as P

DH = 128
WINDOW = 1024
F32 = jnp.float32
BF16 = jnp.bfloat16


def mm(a, b, dims=((1,), (0,))):
    return lax.dot_general(
        a.astype(BF16), b.astype(BF16), (dims, ((), ())), preferred_element_type=F32
    )


def unit_rows(array):
    return array * lax.rsqrt(jnp.sum(array * array, axis=-1, keepdims=True) + 1e-06)


def grids(rows):
    i = lax.broadcasted_iota(jnp.int32, (rows, rows), 0)
    j = lax.broadcasted_iota(jnp.int32, (rows, rows), 1)
    return i, j


def unit_inverses(lowers):
    rows = lowers[0].shape[0]
    i, j = grids(rows)
    apart = i ^ j
    lower = i > j
    first = jnp.where(i == j, 1.0, 0.0)
    inverses = [first - jnp.where(lower & (apart == 1), a, 0.0) for a in lowers]
    level = 1
    while (1 << level) < rows:
        band = lower & ((apart >> level) == 1)
        rounded = [x.astype(BF16) for x in inverses]
        left = [mm(x, jnp.where(band, a, 0.0)) for x, a in zip(rounded, lowers)]
        inverses = [x - mm(y, r) for x, y, r in zip(inverses, left, rounded)]
        level += 1
    return inverses


def delta_local(queries, keys, values, betas, columns, lines):
    heads = range(len(queries))
    rows = queries[0].shape[0]
    i, j = grids(rows)
    ks = [unit_rows(k.astype(F32)) for k in keys]
    qs = [unit_rows(q.astype(F32)) * DH ** (-0.5) for q in queries]
    kb = [k.astype(BF16) for k in ks]
    ratio = [
        jnp.where(i >= j, jnp.exp(jnp.where(i >= j, columns[h] - lines[h], 0.0)), 0.0) for h in heads
    ]
    lowers = [
        jnp.where(i > j, betas[h] * ratio[h] * mm(kb[h], kb[h], ((1,), (1,))), 0.0) for h in heads
    ]
    mixing = [(ratio[h] * mm(qs[h], kb[h], ((1,), (1,)))).astype(BF16) for h in heads]
    inverses = unit_inverses(lowers)
    decayed = [jnp.exp(columns[h]) for h in heads]
    right = [
        jnp.concatenate(
            [values[h].astype(F32) * betas[h], ks[h] * (betas[h] * decayed[h])], axis=1
        )
        for h in heads
    ]
    solved = [mm(inverses[h], right[h]).astype(BF16) for h in heads]
    last = [columns[h][rows - 1 :, :] for h in heads]
    ends = [ks[h] * jnp.exp(last[h] - columns[h]) for h in heads]
    written = [mm(ends[h], solved[h], ((0,), (0,))) for h in heads]
    read = [mm(mixing[h], solved[h]) for h in heads]
    a, b = lax.broadcasted_iota(jnp.int32, (DH, DH), 0), lax.broadcasted_iota(jnp.int32, (DH, DH), 1)
    moves = [
        jnp.where(a == b, jnp.exp(last[h]), 0.0) - written[h][:, DH:] for h in heads
    ]
    adds = [written[h][:, :DH] for h in heads]
    own = [read[h][:, :DH] for h in heads]
    carry = [decayed[h] * qs[h] - read[h][:, DH:] for h in heads]
    return moves, adds, own, carry


def kernel(
    n,
    heads,
    dq, dk, dv, gb, gate, gain, aq, ak, av, wd_any, wa_any,
    out,
    kv, own_out, carry, pair_own, pair_in, joined, s_in, s_out,
    top, den, num, dh, ah, wd, wa, part_out, part_in, kept, sum_out, sum_in,
    w_sem, kv_send, kv_recv, pair_sem, s_sem, part_sem, sum_sem,
):
    c = lax.axis_index("ctx")
    h = lax.axis_index("head")
    odd = lax.rem(c, 2)
    even = 1 - odd
    partner = c + 1 - 2 * odd
    above, below = c + 2, c - 2
    has_up, has_down = above < n, c >= 2
    sibling = h + 1 - 2 * lax.rem(h, 2)
    across = lax.rem(h + 2, 4)
    diagonal = lax.rem(sibling + 2, 4)
    rows = dq.shape[0]

    loads = [
        pltpu.make_async_copy(wd_any, wd, w_sem.at[0]),
        pltpu.make_async_copy(wa_any, wa, w_sem.at[1]),
    ]
    for load in loads:
        load.start()

    barrier = pltpu.get_barrier_semaphore()
    for target in ({"ctx": partner}, {"head": sibling}, {"head": across}):
        pl.semaphore_signal(barrier, inc=1, device_id=target, device_id_type=pl.DeviceIdType.MESH)

    @pl.when(has_up)
    def _():
        pl.semaphore_signal(barrier, inc=1, device_id={"ctx": above}, device_id_type=pl.DeviceIdType.MESH)

    @pl.when(has_down)
    def _():
        pl.semaphore_signal(barrier, inc=1, device_id={"ctx": below}, device_id_type=pl.DeviceIdType.MESH)

    pl.semaphore_wait(barrier, 3 + has_up.astype(jnp.int32) + has_down.astype(jnp.int32))

    def remote(src, dst, send, recv, target):
        return pltpu.make_async_remote_copy(
            src_ref=src, dst_ref=dst, send_sem=send, recv_sem=recv,
            device_id=target, device_id_type=pl.DeviceIdType.MESH,
        )

    def kv_copy(route, part, src, back, target):
        return remote(
            src, kv.at[back - 1, part], kv_send.at[route, part], kv_recv.at[back - 1, part], {"ctx": target}
        )

    mine = (ak, av)

    def routes(part):
        return [
            (has_up, lambda: kv_copy(0, part, mine[part], 2, above)),
            (even == 1, lambda: kv_copy(1, part, mine[part], 1, partner)),
            (has_down & has_up, lambda: kv_copy(2, part, kv.at[1, part], 4, above)),
            (has_down & (even == 1), lambda: kv_copy(3, part, kv.at[1, part], 3, partner)),
            (has_down & (odd == 1), lambda: kv_copy(3, part, kv.at[1, part], 1, partner)),
            ((c >= 4) & (odd == 1), lambda: kv_copy(4, part, kv.at[3, part], 3, partner)),
        ]

    def start(which):
        for part in (0, 1):
            for item in which:
                condition, copy = routes(part)[item]

                @pl.when(condition)
                def _():
                    copy().start()

    def arrived(back, part):
        kv_copy(0, part, mine[part], back, above).wait_recv()

    start((0, 1))

    i, j = grids(rows)
    summed = lax.dot_general(
        jnp.where(i >= j, 1.0, 0.0), gb[...], (((1,), (0,)), ((), ())),
        precision=lax.Precision.HIGHEST, preferred_element_type=F32,
    )
    turned = summed.T

    def cut(ref, head):
        return ref[:, head * DH : (head + 1) * DH]

    for some in ([0, 1], [2, 3]):
        moves, adds, own, carries = delta_local(
            [cut(dq, x) for x in some],
            [cut(dk, x) for x in some],
            [cut(dv, x) for x in some],
            [gb[:, x : x + 1] for x in some],
            [summed[:, heads + x : heads + x + 1] for x in some],
            [turned[heads + x : heads + x + 1, :] for x in some],
        )
        for at, x in enumerate(some):
            pair_own[x, :, :DH] = moves[at].astype(BF16)
            pair_own[x, :, DH:] = adds[at].astype(BF16)
            own_out[x] = own[at]
            carry[x] = carries[at].astype(BF16)

    pair_copy = remote(pair_own, pair_in, pair_sem.at[0], pair_sem.at[1], {"ctx": partner})
    pair_copy.start()

    @pl.when(has_down)
    def _():
        for part in (0, 1):
            arrived(2, part)

    start((2, 3, 4))

    def attend(back):
        keys, vals = mine if back == 0 else (kv.at[back - 1, 0], kv.at[back - 1, 1])
        for x in range(heads):
            scores = mm(cut(aq, x), keys[:, x * DH : (x + 1) * DH], ((1,), (1,))) * DH ** (-0.5)
            if back == 0:
                scores = jnp.where(i >= j, scores, -1e30)
            if back == WINDOW // rows:
                scores = jnp.where(j > i, scores, -1e30)
            block_top = jnp.max(scores, axis=-1, keepdims=True)
            if back == 0:
                high = block_top
            else:
                before = top[x][:, :1]
                high = jnp.maximum(before, block_top)
            weights = jnp.exp(scores - high)
            block_den = jnp.sum(weights, axis=-1, keepdims=True)
            block_num = mm(weights, vals[:, x * DH : (x + 1) * DH])
            if back > 0:
                factor = jnp.exp(before - high)
                block_den = block_den + factor * den[x][:, :1]
                block_num = block_num + factor * num[x]
            top[x] = jnp.broadcast_to(high, (rows, DH))
            den[x] = jnp.broadcast_to(block_den, (rows, DH))
            num[x] = block_num

    attend(0)

    pair_copy.wait_recv()
    for x in range(heads):
        mine_pair, its_pair = pair_own[x].astype(F32), pair_in[x].astype(F32)
        first = jnp.where(even == 1, mine_pair, its_pair)
        second = jnp.where(even == 1, its_pair, mine_pair)
        both = mm(second[:, :DH], first)
        joined[x, :, :DH] = both[:, :DH]
        joined[x, :, DH:] = both[:, DH:] + second[:, DH:]

    state_copy = remote(s_out, s_in, s_sem.at[0], s_sem.at[1], {"ctx": above})

    @pl.when(c < 2)
    def _():
        s_in[...] = jnp.zeros_like(s_in)

    @pl.when(has_up)
    def _():
        @pl.when(has_down)
        def _():
            state_copy.wait_recv()

        for x in range(heads):
            s_out[x] = (mm(joined[x, :, :DH], s_in[x]) + joined[x, :, DH:]).astype(BF16)
        state_copy.start()

    @pl.when(has_down)
    def _():
        attend(2)

    @pl.when(c >= 1)
    def _():
        for part in (0, 1):
            arrived(1, part)
        attend(1)

    @pl.when(c >= 4)
    def _():
        for part in (0, 1):
            arrived(4, part)

    start((5,))

    @pl.when(c >= 4)
    def _():
        attend(4)

    @pl.when(c >= 3)
    def _():
        for part in (0, 1):
            arrived(3, part)
        attend(3)

    for x in range(heads):
        ah[:, x * DH : (x + 1) * DH] = (num[x] / den[x]).astype(BF16)

    @pl.when(has_down & (above >= n))
    def _():
        state_copy.wait_recv()

    for x in range(heads):
        state = s_in[x].astype(F32)
        its_pair = pair_in[x].astype(F32)
        moved = mm(its_pair[:, :DH], state) + its_pair[:, DH:]
        state = jnp.where(odd == 1, moved, state)
        raw = own_out[x] + mm(carry[x], state)
        gates = cut(gate, x).astype(F32)
        scale = lax.rsqrt(jnp.mean(raw * raw, axis=-1, keepdims=True) + 1e-06)
        normed = raw * scale * gain[...] * (gates / (1.0 + jnp.exp(-gates)))
        dh[:, x * DH : (x + 1) * DH] = normed.astype(BF16)

    for load in loads:
        load.wait()
    quarter = rows // 4
    width = out.shape[1]
    tile = 512

    def project(targets, store):
        ds = [pl.ds(pl.multiple_of(t * quarter, quarter), quarter) for t in targets]
        d_rows = jnp.concatenate([dh[d, :] for d in ds], axis=0)
        a_rows = jnp.concatenate([ah[d, :] for d in ds], axis=0)
        for low in range(0, width, tile):
            part = mm(d_rows, wd[:, low : low + tile]) + mm(a_rows, wa[:, low : low + tile])
            for at in range(2):
                store[at, :, low : low + tile] = part[at * quarter : (at + 1) * quarter].astype(BF16)

    project((sibling, diagonal), part_out)
    part_copy = remote(part_out, part_in, part_sem.at[0], part_sem.at[1], {"head": sibling})
    part_copy.start()
    project((h, across), kept)
    part_copy.wait_recv()
    sum_out[...] = (kept[1].astype(F32) + part_in[1].astype(F32)).astype(BF16)
    sum_copy = remote(sum_out, sum_in, sum_sem.at[0], sum_sem.at[1], {"head": across})
    sum_copy.start()
    kept_sum = kept[0].astype(F32) + part_in[0].astype(F32)
    sum_copy.wait_recv()
    out[...] = (kept_sum + sum_in[...].astype(F32)).astype(BF16)

    part_copy.wait_send()
    sum_copy.wait_send()
    pair_copy.wait_send()

    @pl.when(has_up)
    def _():
        state_copy.wait_send()

    for part in (0, 1):
        for condition, copy in routes(part):

            @pl.when(condition)
            def _():
                copy().wait_send()


def shards(
    n,
    delta_q, delta_k, delta_v, beta, log_decay, out_gate, norm_gain,
    attn_q, attn_k, attn_v, w_delta_out, w_attn_out,
):
    rows, columns = delta_q.shape
    heads = columns // DH
    width = w_delta_out.shape[1]
    gb = jnp.concatenate(
        [beta, log_decay, jnp.zeros((rows, DH - 2 * heads), F32)], axis=1
    )
    vmem = pl.BlockSpec(memory_space=pltpu.VMEM)
    hbm = pl.BlockSpec(memory_space=pl.ANY)
    quarter = rows // 4
    return pl.pallas_call(
        functools.partial(kernel, n, heads),
        out_shape=jax.ShapeDtypeStruct((quarter, width), BF16),
        in_specs=[vmem] * 9 + [hbm] * 2,
        out_specs=vmem,
        scratch_shapes=[
            pltpu.VMEM((4, 2, rows, columns), BF16),
            pltpu.VMEM((heads, rows, DH), F32),
            pltpu.VMEM((heads, rows, DH), BF16),
            pltpu.VMEM((heads, DH, 2 * DH), BF16),
            pltpu.VMEM((heads, DH, 2 * DH), BF16),
            pltpu.VMEM((heads, DH, 2 * DH), F32),
            pltpu.VMEM((heads, DH, DH), BF16),
            pltpu.VMEM((heads, DH, DH), BF16),
            pltpu.VMEM((heads, rows, DH), F32),
            pltpu.VMEM((heads, rows, DH), F32),
            pltpu.VMEM((heads, rows, DH), F32),
            pltpu.VMEM((rows, columns), BF16),
            pltpu.VMEM((rows, columns), BF16),
            pltpu.VMEM(w_delta_out.shape, BF16),
            pltpu.VMEM(w_attn_out.shape, BF16),
            pltpu.VMEM((2, quarter, width), BF16),
            pltpu.VMEM((2, quarter, width), BF16),
            pltpu.VMEM((2, quarter, width), BF16),
            pltpu.VMEM((quarter, width), BF16),
            pltpu.VMEM((quarter, width), BF16),
            pltpu.SemaphoreType.DMA((2,)),
            pltpu.SemaphoreType.DMA((5, 2)),
            pltpu.SemaphoreType.DMA((4, 2)),
            pltpu.SemaphoreType.DMA((2,)),
            pltpu.SemaphoreType.DMA((2,)),
            pltpu.SemaphoreType.DMA((2,)),
            pltpu.SemaphoreType.DMA((2,)),
        ],
        compiler_params=pltpu.CompilerParams(
            collective_id=0, has_side_effects=True, vmem_limit_bytes=48 * 1024 * 1024
        ),
        cost_estimate=pl.CostEstimate(flops=4_000_000_000, bytes_accessed=8_000_000, transcendentals=2_000_000),
    )(
        delta_q, delta_k, delta_v, gb, out_gate, norm_gain.reshape(1, DH),
        attn_q, attn_k, attn_v, w_delta_out, w_attn_out,
    )


def solution(mesh):
    return jax.shard_map(
        functools.partial(shards, mesh.shape["ctx"]),
        mesh=mesh,
        in_specs=(
            P("ctx", "head"),
            P("ctx", "head"),
            P("ctx", "head"),
            P("ctx", "head"),
            P("ctx", "head"),
            P("ctx", "head"),
            P(),
            P("ctx", "head"),
            P("ctx", "head"),
            P("ctx", "head"),
            P("head", None),
            P("head", None),
        ),
        out_specs=P(("ctx", "head"), None),
        check_vma=False,
    )
```

```python
import functools

import jax
import jax.numpy as jnp
from jax import lax
from jax.experimental import pallas as pl
from jax.experimental.pallas import tpu as pltpu
from jax.sharding import PartitionSpec as P

DH = 128
WINDOW = 1024
F32 = jnp.float32
BF16 = jnp.bfloat16


def mm(a, b, dims=((1,), (0,))):
    return lax.dot_general(
        a.astype(BF16), b.astype(BF16), (dims, ((), ())), preferred_element_type=F32
    )


def unit_rows(array):
    return array * lax.rsqrt(jnp.sum(array * array, axis=-1, keepdims=True) + 1e-06)


def grids(rows):
    i = lax.broadcasted_iota(jnp.int32, (rows, rows), 0)
    j = lax.broadcasted_iota(jnp.int32, (rows, rows), 1)
    return i, j


def unit_inverses(lowers):
    rows = lowers[0].shape[0]
    i, j = grids(rows)
    apart = i ^ j
    lower = i > j
    first = jnp.where(i == j, 1.0, 0.0)
    inverses = [first - jnp.where(lower & (apart == 1), a, 0.0) for a in lowers]
    level = 1
    while (1 << level) < rows:
        band = lower & ((apart >> level) == 1)
        rounded = [x.astype(BF16) for x in inverses]
        left = [mm(x, jnp.where(band, a, 0.0)) for x, a in zip(rounded, lowers)]
        inverses = [x - mm(y, r) for x, y, r in zip(inverses, left, rounded)]
        level += 1
    return inverses


def delta_local(queries, keys, values, betas, columns, lines):
    heads = range(len(queries))
    rows = queries[0].shape[0]
    i, j = grids(rows)
    ks = [unit_rows(k.astype(F32)) for k in keys]
    qs = [unit_rows(q.astype(F32)) * DH ** (-0.5) for q in queries]
    kb = [k.astype(BF16) for k in ks]
    ratio = [
        jnp.where(i >= j, jnp.exp(jnp.where(i >= j, columns[h] - lines[h], 0.0)), 0.0) for h in heads
    ]
    lowers = [
        jnp.where(i > j, betas[h] * ratio[h] * mm(kb[h], kb[h], ((1,), (1,))), 0.0) for h in heads
    ]
    mixing = [(ratio[h] * mm(qs[h], kb[h], ((1,), (1,)))).astype(BF16) for h in heads]
    inverses = unit_inverses(lowers)
    decayed = [jnp.exp(columns[h]) for h in heads]
    right = [
        jnp.concatenate(
            [values[h].astype(F32) * betas[h], ks[h] * (betas[h] * decayed[h])], axis=1
        )
        for h in heads
    ]
    solved = [mm(inverses[h], right[h]).astype(BF16) for h in heads]
    last = [columns[h][rows - 1 :, :] for h in heads]
    ends = [ks[h] * jnp.exp(last[h] - columns[h]) for h in heads]
    written = [mm(ends[h], solved[h], ((0,), (0,))) for h in heads]
    read = [mm(mixing[h], solved[h]) for h in heads]
    a, b = lax.broadcasted_iota(jnp.int32, (DH, DH), 0), lax.broadcasted_iota(jnp.int32, (DH, DH), 1)
    moves = [
        jnp.where(a == b, jnp.exp(last[h]), 0.0) - written[h][:, DH:] for h in heads
    ]
    adds = [written[h][:, :DH] for h in heads]
    own = [read[h][:, :DH] for h in heads]
    carry = [decayed[h] * qs[h] - read[h][:, DH:] for h in heads]
    return moves, adds, own, carry


def kernel(
    n,
    heads,
    dq_far, dk_far, dv_far, beta_far, rate_far, gate_far, gain_far, aq_far, ak_far, av_far, wd_far, wa_far,
    out,
    dq, dk, dv, beta, rate, gate, gain, aq, ak, av, table,
    kv, own_out, carry, pair_own, pair_in, joined, s_in, s_out,
    top, num, dh, ah, wd, wa, part_out, part_in, kept, sum_out, sum_in,
    w_sem, kv_send, kv_recv, pair_sem, s_sem, part_sem, sum_sem,
):
    c = lax.axis_index("ctx")
    h = lax.axis_index("head")
    odd = lax.rem(c, 2)
    even = 1 - odd
    partner = c + 1 - 2 * odd
    above, below = c + 2, c - 2
    has_up, has_down = above < n, c >= 2
    sibling = h + 1 - 2 * lax.rem(h, 2)
    across = lax.rem(h + 2, 4)
    diagonal = lax.rem(sibling + 2, 4)
    rows = dq.shape[0]

    loads = [
        pltpu.make_async_copy(far, near, w_sem.at[at])
        for at, (far, near) in enumerate(
            (
                (beta_far, beta), (rate_far, rate), (dk_far, dk), (dq_far, dq), (dv_far, dv), (aq_far, aq),
                (ak_far, ak), (av_far, av), (gate_far, gate), (gain_far, gain), (wa_far, wa), (wd_far, wd),
            )
        )
    ]
    for load in loads:
        load.start()

    barrier = pltpu.get_barrier_semaphore()
    for target in ({"ctx": partner}, {"head": sibling}, {"head": across}):
        pl.semaphore_signal(barrier, inc=1, device_id=target, device_id_type=pl.DeviceIdType.MESH)

    @pl.when(has_up)
    def _():
        pl.semaphore_signal(barrier, inc=1, device_id={"ctx": above}, device_id_type=pl.DeviceIdType.MESH)

    @pl.when(has_down)
    def _():
        pl.semaphore_signal(barrier, inc=1, device_id={"ctx": below}, device_id_type=pl.DeviceIdType.MESH)

    pl.semaphore_wait(barrier, 3 + has_up.astype(jnp.int32) + has_down.astype(jnp.int32))

    def remote(src, dst, send, recv, target):
        return pltpu.make_async_remote_copy(
            src_ref=src, dst_ref=dst, send_sem=send, recv_sem=recv,
            device_id=target, device_id_type=pl.DeviceIdType.MESH,
        )

    def kv_copy(route, part, src, back, target):
        return remote(
            src, kv.at[back - 1, part], kv_send.at[route, part], kv_recv.at[back - 1, part], {"ctx": target}
        )

    mine = (ak, av)
    mine_far = (ak_far, av_far)

    def routes(part):
        return [
            (has_up, lambda: kv_copy(0, part, mine_far[part], 2, above)),
            (even == 1, lambda: kv_copy(1, part, mine_far[part], 1, partner)),
            (has_down & has_up, lambda: kv_copy(2, part, kv.at[1, part], 4, above)),
            (has_down & (even == 1), lambda: kv_copy(3, part, kv.at[1, part], 3, partner)),
            (has_down & (odd == 1), lambda: kv_copy(3, part, kv.at[1, part], 1, partner)),
            ((c >= 4) & (odd == 1), lambda: kv_copy(4, part, kv.at[3, part], 3, partner)),
        ]

    def start(which, part):
        for item in which:
            condition, copy = routes(part)[item]

            @pl.when(condition)
            def _():
                copy().start()

    def arrived(back, part):
        kv_copy(0, part, mine_far[part], back, above).wait_recv()

    for part in (0, 1):
        start((0, 1), part)

    i, j = grids(rows)
    for load in loads[:5]:
        load.wait()
    table[...] = jnp.zeros_like(table)
    table[0:heads, :] = beta[...]
    table[8 : 8 + heads, :] = rate[...]
    lines = lax.dot_general(
        table[8:16, :], jnp.where(j >= i, 1.0, 0.0), (((1,), (0,)), ((), ())),
        precision=lax.Precision.HIGHEST, preferred_element_type=F32,
    )
    table[8:16, :] = lines
    turned = table[...].T

    def cut(ref, head):
        return ref[:, head * DH : (head + 1) * DH]

    for some in ([0, 1], [2, 3]):
        moves, adds, own, carries = delta_local(
            [cut(dq, x) for x in some],
            [cut(dk, x) for x in some],
            [cut(dv, x) for x in some],
            [turned[:, x : x + 1] for x in some],
            [turned[:, 8 + x : 9 + x] for x in some],
            [lines[x : x + 1, :] for x in some],
        )
        for at, x in enumerate(some):
            pair_own[x, :, :DH] = moves[at].astype(BF16)
            pair_own[x, :, DH:] = adds[at].astype(BF16)
            own_out[x] = own[at]
            carry[x] = carries[at].astype(BF16)

    pair_copy = remote(pair_own, pair_in, pair_sem.at[0], pair_sem.at[1], {"ctx": partner})
    pair_copy.start()

    for part in (0, 1):

        @pl.when(has_down)
        def _():
            arrived(2, part)

        start((2, 3, 4), part)

    unit = DH ** (-0.5) * 1.4426950408889634
    ones = jnp.ones((rows, DH), BF16)

    def attend(back):
        keys, vals = mine if back == 0 else (kv.at[back - 1, 0], kv.at[back - 1, 1])
        each = range(heads)
        scores = [mm(cut(aq, x), keys[:, x * DH : (x + 1) * DH], ((1,), (1,))) for x in each]
        if back == 0:
            scores = [jnp.where(i >= j, s, -1e30) for s in scores]
        if back == WINDOW // rows:
            scores = [jnp.where(j > i, s, -1e30) for s in scores]
        high = [jnp.max(s, axis=-1, keepdims=True) for s in scores]
        if back > 0:
            before = [top[x] for x in each]
            sums = [num[x] for x in each]
            high = [jnp.maximum(b[:, :1], m) for b, m in zip(before, high)]
        weights = [jnp.exp2((s - m) * unit).astype(BF16) for s, m in zip(scores, high)]
        added = [
            mm(w, jnp.concatenate([vals[:, x * DH : (x + 1) * DH], ones], axis=1))
            for x, w in zip(each, weights)
        ]
        if back > 0:
            factor = [jnp.exp2((b[:, :1] - m) * unit) for b, m in zip(before, high)]
            added = [n + f * o for n, f, o in zip(added, factor, sums)]
        for x in each:
            top[x] = jnp.broadcast_to(high[x], (rows, DH))
            num[x] = added[x]

    for load in loads[5:8]:
        load.wait()
    attend(0)

    pair_copy.wait_recv()
    for x in range(heads):
        mine_pair, its_pair = pair_own[x].astype(F32), pair_in[x].astype(F32)
        first = jnp.where(even == 1, mine_pair, its_pair)
        second = jnp.where(even == 1, its_pair, mine_pair)
        both = mm(second[:, :DH], first)
        joined[x, :, :DH] = both[:, :DH]
        joined[x, :, DH:] = both[:, DH:] + second[:, DH:]

    state_copy = remote(s_out, s_in, s_sem.at[0], s_sem.at[1], {"ctx": above})

    @pl.when(c < 2)
    def _():
        s_in[...] = jnp.zeros_like(s_in)

    def pass_state_up():
        for x in range(heads):
            s_out[x] = (mm(joined[x, :, :DH], s_in[x]) + joined[x, :, DH:]).astype(BF16)
        state_copy.start()

    @pl.when(has_up & (c < 4))
    def _():
        @pl.when(has_down)
        def _():
            state_copy.wait_recv()

        pass_state_up()

    @pl.when(has_down)
    def _():
        attend(2)

    @pl.when(c >= 1)
    def _():
        for part in (0, 1):
            arrived(1, part)
        attend(1)

    for part in (0, 1):

        @pl.when(c >= 4)
        def _():
            arrived(4, part)

        start((5,), part)

    @pl.when(has_up & (c >= 4))
    def _():
        state_copy.wait_recv()
        pass_state_up()

    @pl.when(c >= 4)
    def _():
        attend(4)

    @pl.when(c >= 3)
    def _():
        for part in (0, 1):
            arrived(3, part)
        attend(3)

    for x in range(heads):
        ah[:, x * DH : (x + 1) * DH] = (num[x, :, :DH] / num[x, :, DH:]).astype(BF16)

    @pl.when(has_down & (above >= n))
    def _():
        state_copy.wait_recv()

    for load in loads[8:]:
        load.wait()
    for x in range(heads):
        state = s_in[x].astype(F32)
        its_pair = pair_in[x].astype(F32)
        moved = mm(its_pair[:, :DH], state) + its_pair[:, DH:]
        state = jnp.where(odd == 1, moved, state)
        raw = own_out[x] + mm(carry[x], state)
        gates = cut(gate, x).astype(F32)
        scale = lax.rsqrt(jnp.mean(raw * raw, axis=-1, keepdims=True) + 1e-06)
        normed = raw * scale * gain[...] * (gates / (1.0 + jnp.exp(-gates)))
        dh[:, x * DH : (x + 1) * DH] = normed.astype(BF16)

    quarter = rows // 4
    width = out.shape[1]
    tile = 512

    half = width // 2

    def project(targets, store, side):
        ds = [pl.ds(pl.multiple_of(t * quarter, quarter), quarter) for t in targets]
        d_rows = jnp.concatenate([dh[d, :] for d in ds], axis=0)
        a_rows = jnp.concatenate([ah[d, :] for d in ds], axis=0)
        for low in range(0, half, tile):
            at_col = side * half + low
            part = mm(d_rows, wd[:, at_col : at_col + tile]) + mm(a_rows, wa[:, at_col : at_col + tile])
            for at in range(2):
                store[side, at, :, low : low + tile] = part[at * quarter : (at + 1) * quarter].astype(BF16)

    part_copies = [
        remote(part_out.at[side], part_in.at[side], part_sem.at[0, side], part_sem.at[1, side], {"head": sibling})
        for side in (0, 1)
    ]
    sum_copies = [
        remote(sum_out.at[side], sum_in.at[side], sum_sem.at[0, side], sum_sem.at[1, side], {"head": across})
        for side in (0, 1)
    ]

    def pass_across(side):
        part_copies[side].wait_recv()
        sum_out[side] = (kept[side, 1].astype(F32) + part_in[side, 1].astype(F32)).astype(BF16)
        sum_copies[side].start()

    project((sibling, diagonal), part_out, 0)
    part_copies[0].start()
    project((h, across), kept, 0)
    project((sibling, diagonal), part_out, 1)
    part_copies[1].start()
    pass_across(0)
    project((h, across), kept, 1)
    pass_across(1)
    for side in (0, 1):
        kept_sum = kept[side, 0].astype(F32) + part_in[side, 0].astype(F32)
        sum_copies[side].wait_recv()
        out[:, side * half : (side + 1) * half] = (kept_sum + sum_in[side].astype(F32)).astype(BF16)

    for copy in part_copies + sum_copies:
        copy.wait_send()
    pair_copy.wait_send()

    @pl.when(has_up)
    def _():
        state_copy.wait_send()

    for part in (0, 1):
        for condition, copy in routes(part):

            @pl.when(condition)
            def _():
                copy().wait_send()


def shards(
    n,
    delta_q, delta_k, delta_v, beta, log_decay, out_gate, norm_gain,
    attn_q, attn_k, attn_v, w_delta_out, w_attn_out,
):
    rows, columns = delta_q.shape
    heads = columns // DH
    width = w_delta_out.shape[1]
    vmem = pl.BlockSpec(memory_space=pltpu.VMEM)
    hbm = pl.BlockSpec(memory_space=pltpu.HBM)
    quarter = rows // 4
    return pl.pallas_call(
        functools.partial(kernel, n, heads),
        out_shape=jax.ShapeDtypeStruct((quarter, width), BF16),
        in_specs=[hbm] * 12,
        out_specs=vmem,
        scratch_shapes=[pltpu.VMEM((rows, columns), BF16)] * 3
        + [pltpu.VMEM((heads, rows), F32)] * 2
        + [pltpu.VMEM((rows, columns), BF16), pltpu.VMEM((1, DH), F32)]
        + [pltpu.VMEM((rows, columns), BF16)] * 3
        + [
            pltpu.VMEM((DH, rows), F32),
            pltpu.VMEM((4, 2, rows, columns), BF16),
            pltpu.VMEM((heads, rows, DH), F32),
            pltpu.VMEM((heads, rows, DH), BF16),
            pltpu.VMEM((heads, DH, 2 * DH), BF16),
            pltpu.VMEM((heads, DH, 2 * DH), BF16),
            pltpu.VMEM((heads, DH, 2 * DH), F32),
            pltpu.VMEM((heads, DH, DH), BF16),
            pltpu.VMEM((heads, DH, DH), BF16),
            pltpu.VMEM((heads, rows, DH), F32),
            pltpu.VMEM((heads, rows, 2 * DH), F32),
            pltpu.VMEM((rows, columns), BF16),
            pltpu.VMEM((rows, columns), BF16),
            pltpu.VMEM(w_delta_out.shape, BF16),
            pltpu.VMEM(w_attn_out.shape, BF16),
            pltpu.VMEM((2, 2, quarter, width // 2), BF16),
            pltpu.VMEM((2, 2, quarter, width // 2), BF16),
            pltpu.VMEM((2, 2, quarter, width // 2), BF16),
            pltpu.VMEM((2, quarter, width // 2), BF16),
            pltpu.VMEM((2, quarter, width // 2), BF16),
            pltpu.SemaphoreType.DMA((12,)),
            pltpu.SemaphoreType.DMA((5, 2)),
            pltpu.SemaphoreType.DMA((4, 2)),
            pltpu.SemaphoreType.DMA((2,)),
            pltpu.SemaphoreType.DMA((2,)),
            pltpu.SemaphoreType.DMA((2, 2)),
            pltpu.SemaphoreType.DMA((2, 2)),
        ],
        compiler_params=pltpu.CompilerParams(
            collective_id=0, has_side_effects=True, vmem_limit_bytes=63 * 1024 * 1024
        ),
        cost_estimate=pl.CostEstimate(flops=4_000_000_000, bytes_accessed=8_000_000, transcendentals=2_000_000),
    )(
        delta_q, delta_k, delta_v, beta.T, log_decay.T, out_gate, norm_gain.reshape(1, DH),
        attn_q, attn_k, attn_v, w_delta_out, w_attn_out,
    )


def solution(mesh):
    return jax.shard_map(
        functools.partial(shards, mesh.shape["ctx"]),
        mesh=mesh,
        in_specs=(
            P("ctx", "head"),
            P("ctx", "head"),
            P("ctx", "head"),
            P("ctx", "head"),
            P("ctx", "head"),
            P("ctx", "head"),
            P(),
            P("ctx", "head"),
            P("ctx", "head"),
            P("ctx", "head"),
            P("head", None),
            P("head", None),
        ),
        out_specs=P(("ctx", "head"), None),
        check_vma=False,
    )
```

```python
import functools

import jax
import jax.numpy as jnp
from jax import lax
from jax.experimental import pallas as pl
from jax.experimental.pallas import tpu as pltpu
from jax.sharding import PartitionSpec as P

DH = 128
WINDOW = 1024
F32 = jnp.float32
BF16 = jnp.bfloat16


def mm(a, b, dims=((1,), (0,))):
    return lax.dot_general(
        a.astype(BF16), b.astype(BF16), (dims, ((), ())), preferred_element_type=F32
    )


def unit_rows(array):
    return array * lax.rsqrt(jnp.sum(array * array, axis=-1, keepdims=True) + 1e-06)


def grids(rows):
    i = lax.broadcasted_iota(jnp.int32, (rows, rows), 0)
    j = lax.broadcasted_iota(jnp.int32, (rows, rows), 1)
    return i, j


def unit_inverses(lowers):
    rows = lowers[0].shape[0]
    i, j = grids(rows)
    apart = i ^ j
    lower = i > j
    first = jnp.where(i == j, 1.0, 0.0)
    inverses = [first - jnp.where(lower & (apart == 1), a, 0.0) for a in lowers]
    level = 1
    while (1 << level) < rows:
        band = lower & ((apart >> level) == 1)
        rounded = [x.astype(BF16) for x in inverses]
        left = [mm(x, jnp.where(band, a, 0.0)) for x, a in zip(rounded, lowers)]
        inverses = [x - mm(y, r) for x, y, r in zip(inverses, left, rounded)]
        level += 1
    return inverses


def delta_local(queries, keys, values, betas, columns, lines):
    heads = range(len(queries))
    rows = queries[0].shape[0]
    i, j = grids(rows)
    ks = [unit_rows(k.astype(F32)) for k in keys]
    qs = [unit_rows(q.astype(F32)) * DH ** (-0.5) for q in queries]
    kb = [k.astype(BF16) for k in ks]
    ratio = [
        jnp.where(i >= j, jnp.exp(jnp.where(i >= j, columns[h] - lines[h], 0.0)), 0.0) for h in heads
    ]
    lowers = [
        jnp.where(i > j, betas[h] * ratio[h] * mm(kb[h], kb[h], ((1,), (1,))), 0.0) for h in heads
    ]
    mixing = [(ratio[h] * mm(qs[h], kb[h], ((1,), (1,)))).astype(BF16) for h in heads]
    inverses = unit_inverses(lowers)
    decayed = [jnp.exp(columns[h]) for h in heads]
    right = [
        jnp.concatenate(
            [values[h].astype(F32) * betas[h], ks[h] * (betas[h] * decayed[h])], axis=1
        )
        for h in heads
    ]
    solved = [mm(inverses[h], right[h]).astype(BF16) for h in heads]
    last = [columns[h][rows - 1 :, :] for h in heads]
    ends = [ks[h] * jnp.exp(last[h] - columns[h]) for h in heads]
    written = [mm(ends[h], solved[h], ((0,), (0,))) for h in heads]
    read = [mm(mixing[h], solved[h]) for h in heads]
    a, b = lax.broadcasted_iota(jnp.int32, (DH, DH), 0), lax.broadcasted_iota(jnp.int32, (DH, DH), 1)
    moves = [
        jnp.where(a == b, jnp.exp(last[h]), 0.0) - written[h][:, DH:] for h in heads
    ]
    adds = [written[h][:, :DH] for h in heads]
    own = [read[h][:, :DH] for h in heads]
    carry = [decayed[h] * qs[h] - read[h][:, DH:] for h in heads]
    return moves, adds, own, carry


def kernel(
    n,
    heads,
    dq_far, dk_far, dv_far, beta_far, rate_far, gate_far, gain_far, aq_far, ak_far, av_far, wd_far, wa_far,
    out,
    dq, dk, dv, beta, rate, gate, gain, aq, ak, av, table,
    kv, own_out, carry, pair_own, pair_in, joined, s_in, s_out,
    top, num, dh, ah, wd, wa, part_out, part_in, kept, sum_out, sum_in,
    w_sem, kv_send, kv_recv, pair_sem, s_sem, part_sem, sum_sem,
):
    c = lax.axis_index("ctx")
    h = lax.axis_index("head")
    odd = lax.rem(c, 2)
    even = 1 - odd
    partner = c + 1 - 2 * odd
    above, below = c + 2, c - 2
    has_up, has_down = above < n, c >= 2
    sibling = h + 1 - 2 * lax.rem(h, 2)
    across = lax.rem(h + 2, 4)
    diagonal = lax.rem(sibling + 2, 4)
    rows = dq.shape[0]

    loads = [
        pltpu.make_async_copy(far, near, w_sem.at[at])
        for at, (far, near) in enumerate(
            (
                (beta_far, beta), (rate_far, rate), (dk_far, dk), (dq_far, dq), (dv_far, dv), (aq_far, aq),
                (ak_far, ak), (av_far, av), (gate_far, gate), (gain_far, gain), (wa_far, wa), (wd_far, wd),
            )
        )
    ]
    for load in loads:
        load.start()

    barrier = pltpu.get_barrier_semaphore()
    for target in ({"ctx": partner}, {"head": sibling}, {"head": across}):
        pl.semaphore_signal(barrier, inc=1, device_id=target, device_id_type=pl.DeviceIdType.MESH)

    @pl.when(has_up)
    def _():
        pl.semaphore_signal(barrier, inc=1, device_id={"ctx": above}, device_id_type=pl.DeviceIdType.MESH)

    @pl.when(has_down)
    def _():
        pl.semaphore_signal(barrier, inc=1, device_id={"ctx": below}, device_id_type=pl.DeviceIdType.MESH)

    pl.semaphore_wait(barrier, 3 + has_up.astype(jnp.int32) + has_down.astype(jnp.int32))

    def remote(src, dst, send, recv, target):
        return pltpu.make_async_remote_copy(
            src_ref=src, dst_ref=dst, send_sem=send, recv_sem=recv,
            device_id=target, device_id_type=pl.DeviceIdType.MESH,
        )

    def kv_copy(route, part, src, back, target):
        return remote(
            src, kv.at[back - 1, part], kv_send.at[route, part], kv_recv.at[back - 1, part], {"ctx": target}
        )

    mine = (ak, av)
    mine_far = (ak_far, av_far)

    def routes(part):
        return [
            (has_up, lambda: kv_copy(0, part, mine_far[part], 2, above)),
            (even == 1, lambda: kv_copy(1, part, mine_far[part], 1, partner)),
            (has_down & has_up, lambda: kv_copy(2, part, kv.at[1, part], 4, above)),
            (has_down & (even == 1), lambda: kv_copy(3, part, kv.at[1, part], 3, partner)),
            (has_down & (odd == 1), lambda: kv_copy(3, part, kv.at[1, part], 1, partner)),
            ((c >= 4) & (odd == 1), lambda: kv_copy(4, part, kv.at[3, part], 3, partner)),
        ]

    def start(which, part):
        for item in which:
            condition, copy = routes(part)[item]

            @pl.when(condition)
            def _():
                copy().start()

    def arrived(back, part):
        kv_copy(0, part, mine_far[part], back, above).wait_recv()

    for part in (0, 1):
        start((0, 1), part)

    i, j = grids(rows)
    for load in loads[:5]:
        load.wait()
    table[...] = jnp.zeros_like(table)
    table[0:heads, :] = beta[...]
    table[8 : 8 + heads, :] = rate[...]
    lines = lax.dot_general(
        table[8:16, :], jnp.where(j >= i, 1.0, 0.0), (((1,), (0,)), ((), ())),
        precision=lax.Precision.HIGHEST, preferred_element_type=F32,
    )
    table[8:16, :] = lines
    turned = table[...].T

    def cut(ref, head):
        return ref[:, head * DH : (head + 1) * DH]

    for part, some in enumerate((range(heads // 2), range(heads // 2, heads))):
        moves, adds, own, carries = delta_local(
            [cut(dq, x) for x in some],
            [cut(dk, x) for x in some],
            [cut(dv, x) for x in some],
            [turned[:, x : x + 1] for x in some],
            [turned[:, 8 + x : 9 + x] for x in some],
            [lines[x : x + 1, :] for x in some],
        )
        for at, x in enumerate(some):
            pair_own[x, :, :DH] = moves[at].astype(BF16)
            pair_own[x, :, DH:] = adds[at].astype(BF16)
            own_out[x] = own[at]
            carry[x] = carries[at].astype(BF16)

        @pl.when(has_down)
        def _():
            arrived(2, part)

        start((2, 3, 4), part)

    pair_copy = remote(pair_own, pair_in, pair_sem.at[0], pair_sem.at[1], {"ctx": partner})
    pair_copy.start()

    unit = DH ** (-0.5) * 1.4426950408889634
    ones = jnp.ones((rows, DH), BF16)

    def attend(back):
        keys, vals = mine if back == 0 else (kv.at[back - 1, 0], kv.at[back - 1, 1])
        each = range(heads)
        scores = [mm(cut(aq, x), keys[:, x * DH : (x + 1) * DH], ((1,), (1,))) for x in each]
        if back == 0:
            scores = [jnp.where(i >= j, s, -1e30) for s in scores]
        if back == WINDOW // rows:
            scores = [jnp.where(j > i, s, -1e30) for s in scores]
        high = [jnp.max(s, axis=-1, keepdims=True) for s in scores]
        if back > 0:
            before = [top[x] for x in each]
            sums = [num[x] for x in each]
            high = [jnp.maximum(b[:, :1], m) for b, m in zip(before, high)]
        weights = [jnp.exp2((s - m) * unit).astype(BF16) for s, m in zip(scores, high)]
        added = [
            mm(w, jnp.concatenate([vals[:, x * DH : (x + 1) * DH], ones], axis=1))
            for x, w in zip(each, weights)
        ]
        if back > 0:
            factor = [jnp.exp2((b[:, :1] - m) * unit) for b, m in zip(before, high)]
            added = [n + f * o for n, f, o in zip(added, factor, sums)]
        for x in each:
            top[x] = jnp.broadcast_to(high[x], (rows, DH))
            num[x] = added[x]

    for load in loads[5:8]:
        load.wait()
    attend(0)

    pair_copy.wait_recv()
    for x in range(heads):
        mine_pair, its_pair = pair_own[x].astype(F32), pair_in[x].astype(F32)
        first = jnp.where(even == 1, mine_pair, its_pair)
        second = jnp.where(even == 1, its_pair, mine_pair)
        both = mm(second[:, :DH], first)
        joined[x, :, :DH] = both[:, :DH]
        joined[x, :, DH:] = both[:, DH:] + second[:, DH:]

    state_copy = remote(s_out, s_in, s_sem.at[0], s_sem.at[1], {"ctx": above})

    @pl.when(c < 2)
    def _():
        s_in[...] = jnp.zeros_like(s_in)

    def pass_state_up():
        for x in range(heads):
            s_out[x] = (mm(joined[x, :, :DH], s_in[x]) + joined[x, :, DH:]).astype(BF16)
        state_copy.start()

    @pl.when(has_up & (c < 4))
    def _():
        @pl.when(has_down)
        def _():
            state_copy.wait_recv()

        pass_state_up()

    @pl.when(has_down)
    def _():
        attend(2)

    @pl.when(c >= 1)
    def _():
        for part in (0, 1):
            arrived(1, part)
        attend(1)

    for part in (0, 1):

        @pl.when(c >= 4)
        def _():
            arrived(4, part)

        start((5,), part)

    @pl.when(has_up & (c >= 4))
    def _():
        state_copy.wait_recv()
        pass_state_up()

    @pl.when(c >= 4)
    def _():
        attend(4)

    @pl.when(has_down & (above >= n))
    def _():
        state_copy.wait_recv()

    for load in loads[8:]:
        load.wait()
    for x in range(heads):
        state = s_in[x].astype(F32)
        its_pair = pair_in[x].astype(F32)
        moved = mm(its_pair[:, :DH], state) + its_pair[:, DH:]
        state = jnp.where(odd == 1, moved, state)
        raw = own_out[x] + mm(carry[x], state)
        gates = cut(gate, x).astype(F32)
        scale = lax.rsqrt(jnp.mean(raw * raw, axis=-1, keepdims=True) + 1e-06)
        normed = raw * scale * gain[...] * (gates / (1.0 + jnp.exp(-gates)))
        dh[:, x * DH : (x + 1) * DH] = normed.astype(BF16)

    @pl.when(c >= 3)
    def _():
        for part in (0, 1):
            arrived(3, part)
        attend(3)

    for x in range(heads):
        ah[:, x * DH : (x + 1) * DH] = (num[x, :, :DH] / num[x, :, DH:]).astype(BF16)

    quarter = rows // 4
    width = out.shape[1]
    tile = 512

    half = width // 2

    def project(targets, store, side):
        ds = [pl.ds(pl.multiple_of(t * quarter, quarter), quarter) for t in targets]
        d_rows = jnp.concatenate([dh[d, :] for d in ds], axis=0)
        a_rows = jnp.concatenate([ah[d, :] for d in ds], axis=0)
        for low in range(0, half, tile):
            at_col = side * half + low
            part = mm(d_rows, wd[:, at_col : at_col + tile]) + mm(a_rows, wa[:, at_col : at_col + tile])
            for at in range(2):
                store[side, at, :, low : low + tile] = part[at * quarter : (at + 1) * quarter].astype(BF16)

    part_copies = [
        remote(part_out.at[side], part_in.at[side], part_sem.at[0, side], part_sem.at[1, side], {"head": sibling})
        for side in (0, 1)
    ]
    sum_copies = [
        remote(sum_out.at[side], sum_in.at[side], sum_sem.at[0, side], sum_sem.at[1, side], {"head": across})
        for side in (0, 1)
    ]

    def pass_across(side):
        part_copies[side].wait_recv()
        sum_out[side] = (kept[side, 1].astype(F32) + part_in[side, 1].astype(F32)).astype(BF16)
        sum_copies[side].start()

    project((sibling, diagonal), part_out, 0)
    part_copies[0].start()
    project((h, across), kept, 0)
    project((sibling, diagonal), part_out, 1)
    part_copies[1].start()
    pass_across(0)
    project((h, across), kept, 1)
    pass_across(1)
    for side in (0, 1):
        kept_sum = kept[side, 0].astype(F32) + part_in[side, 0].astype(F32)
        sum_copies[side].wait_recv()
        out[:, side * half : (side + 1) * half] = (kept_sum + sum_in[side].astype(F32)).astype(BF16)

    for copy in part_copies + sum_copies:
        copy.wait_send()
    pair_copy.wait_send()

    @pl.when(has_up)
    def _():
        state_copy.wait_send()

    for part in (0, 1):
        for condition, copy in routes(part):

            @pl.when(condition)
            def _():
                copy().wait_send()


def shards(
    n,
    delta_q, delta_k, delta_v, beta, log_decay, out_gate, norm_gain,
    attn_q, attn_k, attn_v, w_delta_out, w_attn_out,
):
    rows, columns = delta_q.shape
    heads = columns // DH
    width = w_delta_out.shape[1]
    vmem = pl.BlockSpec(memory_space=pltpu.VMEM)
    hbm = pl.BlockSpec(memory_space=pltpu.HBM)
    quarter = rows // 4
    return pl.pallas_call(
        functools.partial(kernel, n, heads),
        out_shape=jax.ShapeDtypeStruct((quarter, width), BF16),
        in_specs=[hbm] * 12,
        out_specs=vmem,
        scratch_shapes=[pltpu.VMEM((rows, columns), BF16)] * 3
        + [pltpu.VMEM((heads, rows), F32)] * 2
        + [pltpu.VMEM((rows, columns), BF16), pltpu.VMEM((1, DH), F32)]
        + [pltpu.VMEM((rows, columns), BF16)] * 3
        + [
            pltpu.VMEM((DH, rows), F32),
            pltpu.VMEM((4, 2, rows, columns), BF16),
            pltpu.VMEM((heads, rows, DH), F32),
            pltpu.VMEM((heads, rows, DH), BF16),
            pltpu.VMEM((heads, DH, 2 * DH), BF16),
            pltpu.VMEM((heads, DH, 2 * DH), BF16),
            pltpu.VMEM((heads, DH, 2 * DH), F32),
            pltpu.VMEM((heads, DH, DH), BF16),
            pltpu.VMEM((heads, DH, DH), BF16),
            pltpu.VMEM((heads, rows, DH), F32),
            pltpu.VMEM((heads, rows, 2 * DH), F32),
            pltpu.VMEM((rows, columns), BF16),
            pltpu.VMEM((rows, columns), BF16),
            pltpu.VMEM(w_delta_out.shape, BF16),
            pltpu.VMEM(w_attn_out.shape, BF16),
            pltpu.VMEM((2, 2, quarter, width // 2), BF16),
            pltpu.VMEM((2, 2, quarter, width // 2), BF16),
            pltpu.VMEM((2, 2, quarter, width // 2), BF16),
            pltpu.VMEM((2, quarter, width // 2), BF16),
            pltpu.VMEM((2, quarter, width // 2), BF16),
            pltpu.SemaphoreType.DMA((12,)),
            pltpu.SemaphoreType.DMA((5, 2)),
            pltpu.SemaphoreType.DMA((4, 2)),
            pltpu.SemaphoreType.DMA((2,)),
            pltpu.SemaphoreType.DMA((2,)),
            pltpu.SemaphoreType.DMA((2, 2)),
            pltpu.SemaphoreType.DMA((2, 2)),
        ],
        compiler_params=pltpu.CompilerParams(
            collective_id=0, has_side_effects=True, vmem_limit_bytes=63 * 1024 * 1024
        ),
        cost_estimate=pl.CostEstimate(flops=4_000_000_000, bytes_accessed=8_000_000, transcendentals=2_000_000),
    )(
        delta_q, delta_k, delta_v, beta.T, log_decay.T, out_gate, norm_gain.reshape(1, DH),
        attn_q, attn_k, attn_v, w_delta_out, w_attn_out,
    )


def solution(mesh):
    return jax.shard_map(
        functools.partial(shards, mesh.shape["ctx"]),
        mesh=mesh,
        in_specs=(
            P("ctx", "head"),
            P("ctx", "head"),
            P("ctx", "head"),
            P("ctx", "head"),
            P("ctx", "head"),
            P("ctx", "head"),
            P(),
            P("ctx", "head"),
            P("ctx", "head"),
            P("ctx", "head"),
            P("head", None),
            P("head", None),
        ),
        out_specs=P(("ctx", "head"), None),
        check_vma=False,
    )
```
